32 devices in a mesh: band: 4 (over y, x), grid: 8 (over z, core).
Axes of the slice: x: 2, y: 2, z: 4, core: 2. Of those that a mesh axis runs over, the one named last changes fastest.
Arguments:
- orbitals: float32 [640, 12288], P('band', 'grid'), may hold values from -6 to 6
Outputs:
- corrected: float32 [640, 12288], P('band', 'grid')
The draws below stay inside these ranges and needn't reach their ends.
All inputs are finite; a program needn't handle non-finite values.
Results may differ from the reference program's by a relative error of at most 0.0001.
Values sent between devices are 32-bit elements; how exact they have to be, the bound alone decides.
A program may use at most 64 MiB of HBM per device.

```python
import jax
import jax.numpy as jnp
from jax import lax

BD = 160
NB = 640
NG = 12288
SHIFTS = 1
N_BAND = 4


def shard_levels(stream_key, shape, pieces, low, high):
    loudness, own = 1.0, jax.random.fold_in(stream_key, 6)
    for dim, blocks in pieces:
        steps = jnp.exp(jax.random.uniform(jax.random.fold_in(own, dim), (blocks,), jnp.float32, low / len(pieces), high / len(pieces)))
        loudness = loudness * jnp.repeat(steps, shape[dim] // blocks).reshape([-1 if axis == dim else 1 for axis in range(len(shape))])
    return loudness


def noise(key, extent, deviation, reach, split=(), kind=jnp.bfloat16):
    entries = jax.random.normal(key, extent, jnp.float32) * deviation
    if len(split) > 0:
        entries = shard_levels(key, extent, split, -0.22, 0.18) * entries
    return jnp.clip(entries, min=-reach, max=reach).astype(kind)


def setup_inputs(seed: int = 0) -> dict:
    splits = jax.random.split(jax.random.key(seed), 2)
    orbitals = noise(splits[0], (NB, NG), 1.0, 6.0, ((0, 4), (1, 8)), jnp.float32)
    return dict(orbitals=orbitals)


def reference(orbitals):
    highest = lax.Precision.HIGHEST
    blocks = orbitals.reshape(N_BAND, BD, NG)
    identity = jnp.eye(BD, dtype=jnp.float32)

    def correlation(left, right):
        return jnp.einsum("bin,bjn->bij", left, right, precision=highest) / NG

    tile = correlation(blocks, blocks)
    fix = jnp.einsum("bij,bjn->bin", tile - identity, blocks, precision=highest)
    for shift_count in range(1, SHIFTS + 1):
        other = jnp.roll(blocks, shift_count, axis=0)
        tile = correlation(blocks, other)
        fix = fix + jnp.einsum("bij,bjn->bin", tile, other, precision=highest)
        backward = jnp.einsum("bji,bjn->bin", tile, blocks, precision=highest)
        fix = fix + jnp.roll(backward, -shift_count, axis=0)
    return orbitals - 0.5 * fix.reshape(N_BAND * BD, NG)
```

```python
import functools

import jax
import jax.numpy as jnp
from jax import lax
from jax.experimental import pallas as pl
from jax.experimental.pallas import tpu as pltpu
from jax.sharding import PartitionSpec as P

MESH = pl.DeviceIdType.MESH
NT = (((1,), (1,)), ((), ()))
NN = (((1,), (0,)), ((), ()))


def passed_along(block, axis, distance):
    devices = range(lax.axis_size(axis))
    route = [((i - distance) % len(devices), i) for i in devices]
    return lax.ppermute(block, axis, route)


def product(left, right):
    return jnp.dot(left, right, precision=lax.Precision.HIGHEST, preferred_element_type=jnp.float32)


def general_shards(orbitals):
    band_count = lax.axis_size("band")
    shifts = min(4, (band_count - 1) // 2)
    points = orbitals.shape[1] * lax.axis_size("grid")
    others = []
    for distance in range(1, shifts + 1):
        others.append(passed_along(orbitals, "band", distance))
    neighbours = [orbitals] + others
    partials = [product(orbitals, other.T) for other in neighbours]
    tiles = [lax.psum(partial_value, "grid") / points for partial_value in partials]
    identity = jnp.eye(orbitals.shape[0], dtype=jnp.float32)
    fix = product(tiles[0] - identity, orbitals)
    terms = [None]
    for distance in range(1, shifts + 1):
        fix = fix + product(tiles[distance], others[distance - 1])
        terms.append(product(tiles[distance].T, orbitals))
    for distance in range(1, shifts + 1):
        fix = fix + passed_along(terms[distance], "band", -distance)
    return orbitals - 0.5 * fix


def split(a):
    hi = a.astype(jnp.bfloat16)
    return hi, (a - hi.astype(jnp.float32)).astype(jnp.bfloat16)


def mm(a, b, dims):
    dot = functools.partial(lax.dot_general, dimension_numbers=dims, preferred_element_type=jnp.float32)
    return dot(a[0], b[0]) + (dot(a[0], b[1]) + dot(a[1], b[0]))


def kernel(
    nr, width, depth, x_ref, o_ref,
    blocks, dpart, drs, dred, dfull, tpart, tcore, trs, tred, tpair, tfull, fix,
    own_sem, xs, xr, ys, yr, drss, drsr, dags, dagr, cs, cr, rss, rsr, ps, pr, ags, agr, fs, fr, os,
):
    bd, cols = x_ref.shape
    nz = nr // 2
    points = cols * nr
    half = cols // 2
    n = cols // width
    nh = n // 2
    g = lax.axis_index("band")
    r = lax.axis_index("grid")
    z, core = r // 2, r % 2
    par = g % 2
    xn, yn, dn = g + 1 - 2 * par, (g + 2) % 4, 3 - g
    mate = z * 2 + (1 - core)
    partner = xn * (1 - core) + dn * core

    own_copy = pltpu.make_async_copy(x_ref, blocks.at[pl.ds(0, bd)], own_sem)
    own_copy.start()

    barrier = pltpu.get_barrier_semaphore()
    for peer in (xn, yn, dn):
        pl.semaphore_signal(barrier, inc=1, device_id={"band": peer}, device_id_type=MESH)
    for k in range(1, nr):
        pl.semaphore_signal(barrier, inc=1, device_id={"grid": (r + k) % nr}, device_id_type=MESH)
    pl.semaphore_wait(barrier, 3 + nr - 1)

    def columns(c, parity):
        start = parity * half + c * width
        start = lax.rem(start, cols)
        return pl.ds(pl.multiple_of(start, 128), width)

    def remote(src, dst, send, recv, where):
        return pltpu.make_async_remote_copy(
            src_ref=src, dst_ref=dst, send_sem=send, recv_sem=recv, device_id=where, device_id_type=MESH)

    def x_send(c):
        at = columns(c, 1 - par)
        return remote(x_ref.at[:, at], blocks.at[pl.ds(bd, bd), at], xs.at[c], xr.at[c], {"band": xn})

    def x_recv(c):
        at = columns(c, par)
        return remote(x_ref.at[:, at], blocks.at[pl.ds(bd, bd), at], xs.at[c], xr.at[c], {"band": xn})

    def y_copy(c):
        at = columns(c, par)
        return remote(blocks.at[pl.ds(bd, bd), at], blocks.at[pl.ds(2 * bd, bd), at], ys.at[c], yr.at[c], {"band": yn})

    for c in range(min(depth, n)):
        x_send(c).start()

    own_copy.wait()

    def step_x(c):
        x_recv(c).wait_recv()
        y_copy(c).start()
        x_send(c).wait_send()
        if c + depth < n:
            x_send(c + depth).start()

    mine = split(blocks[pl.ds(0, bd), :])
    own_tile = mm(mine, mine, NT)
    rows = bd // nr
    for j in range(nr):
        dpart[j] = own_tile[j * rows:(j + 1) * rows]

    def drs_copy(k):
        return remote(dpart.at[(r + k) % nr], drs.at[k - 1], drss.at[k - 1], drsr.at[k - 1], {"grid": (r + k) % nr})

    def dag_copy(k):
        return remote(dred, dfull.at[r], dags.at[k - 1], dagr.at[k - 1], {"grid": (r + k) % nr})

    def dag_arrival(k):
        return remote(dred, dfull.at[(r + nr - k) % nr], dags.at[k - 1], dagr.at[k - 1], {"grid": (r + k) % nr})

    for k in range(1, nr):
        drs_copy(k).start()

    def add_tile(which, c):
        at = columns(c, par)
        a = split(blocks[pl.ds(0, bd), at])
        b = split(blocks[pl.ds((1 + which) * bd, bd), at])

        @pl.when(par == 0)
        def _():
            value = mm(a, b, NT).reshape(nz, bd // nz, bd)
            tpart[which] = value if c == 0 else tpart[which] + value

        @pl.when(par == 1)
        def _():
            value = mm(b, a, NT).reshape(nz, bd // nz, bd)
            tpart[which] = value if c == 0 else tpart[which] + value

    for c in range(nh):
        step_x(c)
        add_tile(0, c)
        if c >= 1:
            y_copy(c - 1).wait_recv()
            add_tile(1, c - 1)
        if c == 1:
            for k in range(1, nr):
                drs_copy(k).wait_recv()
            total = dpart[r]
            for k in range(1, nr):
                total = total + drs[k - 1]
            dred[...] = total
            dfull[r] = total
            for k in range(1, nr):
                dag_copy(k).start()

    core_copy = remote(tpart.at[1 - core], tcore, cs, cr, {"grid": mate})

    @pl.when(core == 1)
    def _():
        core_copy.start()

    step_x(nh)
    y_copy(nh - 1).wait_recv()
    add_tile(1, nh - 1)

    @pl.when(core == 0)
    def _():
        core_copy.start()

    def other_z(k):
        return lax.rem(z + k, nz)

    def rs_copy(k):
        return remote(tcore.at[other_z(k)], trs.at[k - 1], rss.at[k - 1], rsr.at[k - 1], {"grid": other_z(k) * 2 + core})

    core_copy.wait()
    tcore[...] = tcore[...] + tpart[core]
    for k in range(1, nz):
        rs_copy(k).start()
    step_x(nh + 1)
    step_x(nh + 2)
    for k in range(1, nz):
        rs_copy(k).wait_recv()
    total = tcore[z]
    for k in range(1, nz):
        total = total + trs[k - 1]
    tred[...] = total
    pair_copy = remote(tred, tpair, ps, pr, {"band": partner})
    pair_copy.start()
    for c in range(nh + 3, n - 1):
        step_x(c)
    pair_copy.wait()
    total = tred[...] + tpair[...]
    tfull[core, z] = total

    def ag_copy(k):
        return remote(tfull.at[core, z], tfull.at[core, z], ags.at[k - 1], agr.at[k - 1], {"grid": other_z(k) * 2 + core})

    def ag_arrival(k):
        at = tfull.at[core, lax.rem(z + nz - k, nz)]
        return remote(at, at, ags.at[k - 1], agr.at[k - 1], {"grid": other_z(k) * 2 + core})

    def mate_copy(k):
        at = tfull.at[core, lax.rem(z + nz - k, nz)]
        return remote(at, at, fs.at[k], fr.at[k], {"grid": mate})

    def mate_arrival(k):
        at = tfull.at[1 - core, lax.rem(z + nz - k, nz)]
        return remote(at, at, fs.at[k], fr.at[k], {"grid": mate})

    for k in range(1, nz):
        ag_copy(k).start()
    mate_copy(0).start()
    step_x(n - 1)

    for k in range(1, nr):
        dag_arrival(k).wait_recv()
    scale = -0.5 / points
    own_w = split(jnp.concatenate([dfull[j] for j in range(nr)], axis=0) * scale)
    wide = 2 * width
    for t in range(cols // wide):
        at = pl.ds(t * wide, wide)
        a = blocks[pl.ds(0, bd), at]
        fix[:, at] = 1.5 * a + mm(own_w, split(a), NN)

    for k in range(1, nz):
        ag_arrival(k).wait_recv()
        mate_copy(k).start()
    for c in range(nh, n):
        y_copy(c).wait_recv()
    for k in range(nz):
        mate_arrival(k).wait_recv()

    @pl.when(par == 1)
    def _():
        for which in range(2):
            tpart[which] = tfull[which].reshape(bd, bd).T.reshape(nz, bd // nz, bd)

    @pl.when(par == 0)
    def _():
        for which in range(2):
            tpart[which] = tfull[which]

    w0 = split(tpart[0].reshape(bd, bd) * scale)
    w1 = split(tpart[1].reshape(bd, bd) * scale)
    outs = []
    for t in range(cols // wide):
        at = pl.ds(t * wide, wide)
        b0 = split(blocks[pl.ds(bd, bd), at])
        b1 = split(blocks[pl.ds(2 * bd, bd), at])
        fix[:, at] = fix[:, at] + (mm(w0, b0, NN) + mm(w1, b1, NN))
        outs.append(pltpu.make_async_copy(fix.at[:, at], o_ref.at[:, at], os.at[t]))
        outs[-1].start()

    for c in range(n):
        y_copy(c).wait_send()
    for k in range(1, nr):
        drs_copy(k).wait_send()
        dag_copy(k).wait_send()
    for k in range(1, nz):
        rs_copy(k).wait_send()
        ag_copy(k).wait_send()
    for k in range(nz):
        mate_copy(k).wait_send()
    for copy in outs:
        copy.wait()


def paired_shards(orbitals):
    bd, cols = orbitals.shape
    nr = lax.axis_size("grid")
    nz = nr // 2
    width = 128
    n = cols // width
    f32 = jnp.float32
    dma = pltpu.SemaphoreType.DMA
    rows = bd // nr
    part = bd // nz
    return pl.pallas_call(
        functools.partial(kernel, nr, width, 3),
        out_shape=jax.ShapeDtypeStruct((bd, cols), f32),
        in_specs=[pl.BlockSpec(memory_space=pl.ANY)],
        out_specs=pl.BlockSpec(memory_space=pl.ANY),
        scratch_shapes=[
            pltpu.VMEM((3 * bd, cols), f32),
            pltpu.VMEM((nr, rows, bd), f32),
            pltpu.VMEM((nr - 1, rows, bd), f32),
            pltpu.VMEM((rows, bd), f32),
            pltpu.VMEM((nr, rows, bd), f32),
            pltpu.VMEM((2, nz, part, bd), f32),
            pltpu.VMEM((nz, part, bd), f32),
            pltpu.VMEM((nz - 1, part, bd), f32),
            pltpu.VMEM((part, bd), f32),
            pltpu.VMEM((part, bd), f32),
            pltpu.VMEM((2, nz, part, bd), f32),
            pltpu.VMEM((bd, cols), f32),
            dma, dma((n,)), dma((n,)), dma((n,)), dma((n,)),
            dma((nr - 1,)), dma((nr - 1,)), dma((nr - 1,)), dma((nr - 1,)),
            dma, dma, dma((nz - 1,)), dma((nz - 1,)), dma, dma,
            dma((nz - 1,)), dma((nz - 1,)), dma((nz,)), dma((nz,)),
            dma((n // 2,)),
        ],
        compiler_params=pltpu.CompilerParams(
            collective_id=0, has_side_effects=True, vmem_limit_bytes=32 * 1024 * 1024),
        cost_estimate=pl.CostEstimate(
            flops=12 * bd * bd * cols, bytes_accessed=8 * bd * cols, transcendentals=0),
    )(orbitals)


def shards(orbitals):
    bd, cols = orbitals.shape
    nr = lax.axis_size("grid")
    fits = nr % 2 == 0 and nr >= 4 and bd % (4 * nr) == 0 and cols % 256 == 0 and cols >= 2048 // 2
    if lax.axis_size("band") == 4 and fits:
        return paired_shards(orbitals)
    return general_shards(orbitals)


def solution(mesh):
    return jax.shard_map(
        shards,
        mesh=mesh,
        in_specs=(P("band", "grid"),),
        out_specs=P("band", "grid"),
        check_vma=False,
    )
```

```python
import functools

import jax
import jax.numpy as jnp
from jax import lax
from jax.experimental import pallas as pl
from jax.experimental.pallas import tpu as pltpu
from jax.sharding import PartitionSpec as P

MESH = pl.DeviceIdType.MESH
NT = (((1,), (1,)), ((), ()))
NN = (((1,), (0,)), ((), ()))


def passed_along(block, axis, distance):
    devices = range(lax.axis_size(axis))
    route = [((i - distance) % len(devices), i) for i in devices]
    return lax.ppermute(block, axis, route)


def product(left, right):
    return jnp.dot(left, right, precision=lax.Precision.HIGHEST, preferred_element_type=jnp.float32)


def general_shards(orbitals):
    band_count = lax.axis_size("band")
    shifts = min(4, (band_count - 1) // 2)
    points = orbitals.shape[1] * lax.axis_size("grid")
    others = []
    for distance in range(1, shifts + 1):
        others.append(passed_along(orbitals, "band", distance))
    neighbours = [orbitals] + others
    partials = [product(orbitals, other.T) for other in neighbours]
    tiles = [lax.psum(partial_value, "grid") / points for partial_value in partials]
    identity = jnp.eye(orbitals.shape[0], dtype=jnp.float32)
    fix = product(tiles[0] - identity, orbitals)
    terms = [None]
    for distance in range(1, shifts + 1):
        fix = fix + product(tiles[distance], others[distance - 1])
        terms.append(product(tiles[distance].T, orbitals))
    for distance in range(1, shifts + 1):
        fix = fix + passed_along(terms[distance], "band", -distance)
    return orbitals - 0.5 * fix


def split(a):
    hi = a.astype(jnp.bfloat16)
    return hi, (a - hi.astype(jnp.float32)).astype(jnp.bfloat16)


def mm(a, b, dims):
    dot = functools.partial(lax.dot_general, dimension_numbers=dims, preferred_element_type=jnp.float32)
    return dot(a[0], b[0]) + (dot(a[0], b[1]) + dot(a[1], b[0]))


def kernel(
    nr, width, depth, x_ref, o_ref,
    blocks, dpart, dcore, drs, dred, dfull, tpart, tcore, trs, tred, tpair, tfull, fix,
    own_sem, xs, xr, ys, yr, dcs, dcr, drss, drsr, dags, dagr, cs, cr, rss, rsr, ps, pr, ags, agr, fs, fr, os,
):
    bd, cols = x_ref.shape
    nz = nr // 2
    points = cols * nr
    half = cols // 2
    n = cols // width
    nh = n // 2
    g = lax.axis_index("band")
    r = lax.axis_index("grid")
    z, core = r // 2, r % 2
    par = g % 2
    xn, yn, dn = g + 1 - 2 * par, (g + 2) % 4, 3 - g
    mate = z * 2 + (1 - core)
    partner = xn * (1 - core) + dn * core

    own_copy = pltpu.make_async_copy(x_ref, blocks.at[pl.ds(0, bd)], own_sem)
    own_copy.start()

    barrier = pltpu.get_barrier_semaphore()
    for peer in (xn, yn, dn):
        pl.semaphore_signal(barrier, inc=1, device_id={"band": peer}, device_id_type=MESH)
    pl.semaphore_signal(barrier, inc=1, device_id={"grid": mate}, device_id_type=MESH)
    for k in range(1, nz):
        pl.semaphore_signal(
            barrier, inc=1, device_id={"grid": lax.rem(z + k, nz) * 2 + core}, device_id_type=MESH)
    pl.semaphore_wait(barrier, 4 + nz - 1)

    def columns(c, parity):
        start = parity * half + c * width
        start = lax.rem(start, cols)
        return pl.ds(pl.multiple_of(start, 128), width)

    def remote(src, dst, send, recv, where):
        return pltpu.make_async_remote_copy(
            src_ref=src, dst_ref=dst, send_sem=send, recv_sem=recv, device_id=where, device_id_type=MESH)

    def x_send(c):
        at = columns(c, 1 - par)
        return remote(x_ref.at[:, at], blocks.at[pl.ds(bd, bd), at], xs.at[c], xr.at[c], {"band": xn})

    def x_recv(c):
        at = columns(c, par)
        return remote(x_ref.at[:, at], blocks.at[pl.ds(bd, bd), at], xs.at[c], xr.at[c], {"band": xn})

    def y_copy(c):
        at = columns(c, par)
        return remote(blocks.at[pl.ds(bd, bd), at], blocks.at[pl.ds(2 * bd, bd), at], ys.at[c], yr.at[c], {"band": yn})

    for c in range(min(depth, n)):
        x_send(c).start()

    own_copy.wait()

    def step_x(c):
        x_recv(c).wait_recv()
        y_copy(c).start()
        x_send(c).wait_send()
        if c + depth < n:
            x_send(c + depth).start()

    mine = split(blocks[pl.ds(0, bd), :])
    dpart[...] = mm(mine, mine, NT).reshape(nz, bd // nz, bd)

    def other_z(k):
        return lax.rem(z + k, nz)

    def to_z(k):
        return {"grid": other_z(k) * 2 + core}

    def drs_copy(k):
        return remote(dcore.at[other_z(k)], drs.at[k - 1], drss.at[k - 1], drsr.at[k - 1], to_z(k))

    def dag_copy(k):
        return remote(dred, dfull.at[z], dags.at[k - 1], dagr.at[k - 1], to_z(k))

    def dag_arrival(k):
        return remote(dred, dfull.at[lax.rem(z + nz - k, nz)], dags.at[k - 1], dagr.at[k - 1], to_z(k))

    dcore_copy = remote(dpart, dcore, dcs, dcr, {"grid": mate})
    dcore_copy.start()

    def add_tile(which, c):
        at = columns(c, par)
        a = split(blocks[pl.ds(0, bd), at])
        b = split(blocks[pl.ds((1 + which) * bd, bd), at])

        @pl.when(par == 0)
        def _():
            value = mm(a, b, NT).reshape(nz, bd // nz, bd)
            tpart[which] = value if c == 0 else tpart[which] + value

        @pl.when(par == 1)
        def _():
            value = mm(b, a, NT).reshape(nz, bd // nz, bd)
            tpart[which] = value if c == 0 else tpart[which] + value

    for c in range(nh):
        step_x(c)
        add_tile(0, c)
        if c >= 1:
            y_copy(c - 1).wait_recv()
            add_tile(1, c - 1)
        if c == 0:
            dcore_copy.wait()
            dcore[...] = dcore[...] + dpart[...]
            for k in range(1, nz):
                drs_copy(k).start()
        if c == 2:
            for k in range(1, nz):
                drs_copy(k).wait_recv()
            total = dcore[z]
            for k in range(1, nz):
                total = total + drs[k - 1]
            dred[...] = total
            dfull[z] = total
            for k in range(1, nz):
                dag_copy(k).start()

    core_copy = remote(tpart.at[1 - core], tcore, cs, cr, {"grid": mate})
    pair_copy = remote(tred, tpair, ps, pr, {"band": partner})

    def rs_copy(k):
        return remote(tcore.at[other_z(k)], trs.at[k - 1], rss.at[k - 1], rsr.at[k - 1], to_z(k))

    def ag_copy(k):
        return remote(tfull.at[core, z], tfull.at[core, z], ags.at[k - 1], agr.at[k - 1], {"grid": other_z(k) * 2 + core})

    def ag_arrival(k):
        at = tfull.at[core, lax.rem(z + nz - k, nz)]
        return remote(at, at, ags.at[k - 1], agr.at[k - 1], {"grid": other_z(k) * 2 + core})

    def mate_copy(k):
        at = tfull.at[core, lax.rem(z + nz - k, nz)]
        return remote(at, at, fs.at[k], fr.at[k], {"grid": mate})

    def mate_arrival(k):
        at = tfull.at[1 - core, lax.rem(z + nz - k, nz)]
        return remote(at, at, fs.at[k], fr.at[k], {"grid": mate})

    def on(which, stage):
        @pl.when(core == which)
        def _():
            stage()

    def sum_cores():
        core_copy.wait_recv()
        tcore[...] = tcore[...] + tpart[core]
        for k in range(1, nz):
            rs_copy(k).start()

    def sum_z():
        for k in range(1, nz):
            rs_copy(k).wait_recv()
        total = tcore[z]
        for k in range(1, nz):
            total = total + trs[k - 1]
        tred[...] = total
        pair_copy.start()

    def sum_pair():
        pair_copy.wait_recv()
        tfull[core, z] = tred[...] + tpair[...]
        for k in range(1, nz):
            ag_copy(k).start()
        mate_copy(0).start()

    def pass_on():
        for k in range(1, nz):
            ag_arrival(k).wait_recv()
            mate_copy(k).start()

    def from_mate():
        for k in range(nz):
            mate_arrival(k).wait_recv()

    on(1, core_copy.start)
    on(0, sum_cores)
    step_x(nh)
    y_copy(nh - 1).wait_recv()
    add_tile(1, nh - 1)
    on(0, core_copy.start)
    on(1, sum_cores)
    on(0, sum_z)
    for c in range(nh + 1, nh + 4):
        if c < n:
            step_x(c)
    on(0, sum_pair)
    for c in range(nh + 4, n - 1):
        step_x(c)
    on(1, sum_z)
    for c in range(max(n - 1, nh + 4), n):
        step_x(c)
    on(1, sum_pair)

    for k in range(1, nz):
        dag_arrival(k).wait_recv()
    scale = -0.5 / points
    wide = 2 * width
    steps = [pl.ds(t * wide, wide) for t in range(cols // wide)]
    on(0, pass_on)
    own_w = split(dfull[...].reshape(bd, bd) * scale)
    for at in steps:
        a = blocks[pl.ds(0, bd), at]
        fix[:, at] = 1.5 * a + mm(own_w, split(a), NN)
    core_copy.wait_send()

    def weights(which):
        @pl.when(par == 1)
        def _():
            tpart[which] = tfull[which].reshape(bd, bd).T.reshape(nz, bd // nz, bd)

        @pl.when(par == 0)
        def _():
            tpart[which] = tfull[which]

        return split(tpart[which].reshape(bd, bd) * scale)

    on(1, from_mate)
    w0 = weights(0)
    for at in steps:
        fix[:, at] = fix[:, at] + mm(w0, split(blocks[pl.ds(bd, bd), at]), NN)

    on(1, pass_on)
    for c in range(nh, n):
        y_copy(c).wait_recv()
    on(0, from_mate)
    w1 = weights(1)
    outs = []
    for t, at in enumerate(steps):
        fix[:, at] = fix[:, at] + mm(w1, split(blocks[pl.ds(2 * bd, bd), at]), NN)
        outs.append(pltpu.make_async_copy(fix.at[:, at], o_ref.at[:, at], os.at[t]))
        outs[-1].start()

    for c in range(n):
        y_copy(c).wait_send()
    pair_copy.wait_send()
    for k in range(1, nz):
        drs_copy(k).wait_send()
        dag_copy(k).wait_send()
        rs_copy(k).wait_send()
        ag_copy(k).wait_send()
    for k in range(nz):
        mate_copy(k).wait_send()
    for copy in outs:
        copy.wait()


def paired_shards(orbitals):
    bd, cols = orbitals.shape
    nr = lax.axis_size("grid")
    nz = nr // 2
    width = 128
    n = cols // width
    f32 = jnp.float32
    dma = pltpu.SemaphoreType.DMA
    part = bd // nz
    return pl.pallas_call(
        functools.partial(kernel, nr, width, 3),
        out_shape=jax.ShapeDtypeStruct((bd, cols), f32),
        in_specs=[pl.BlockSpec(memory_space=pl.ANY)],
        out_specs=pl.BlockSpec(memory_space=pl.ANY),
        scratch_shapes=[
            pltpu.VMEM((3 * bd, cols), f32),
            pltpu.VMEM((nz, part, bd), f32),
            pltpu.VMEM((nz, part, bd), f32),
            pltpu.VMEM((nz - 1, part, bd), f32),
            pltpu.VMEM((part, bd), f32),
            pltpu.VMEM((nz, part, bd), f32),
            pltpu.VMEM((2, nz, part, bd), f32),
            pltpu.VMEM((nz, part, bd), f32),
            pltpu.VMEM((nz - 1, part, bd), f32),
            pltpu.VMEM((part, bd), f32),
            pltpu.VMEM((part, bd), f32),
            pltpu.VMEM((2, nz, part, bd), f32),
            pltpu.VMEM((bd, cols), f32),
            dma, dma((n,)), dma((n,)), dma((n,)), dma((n,)),
            dma, dma, dma((nz - 1,)), dma((nz - 1,)), dma((nz - 1,)), dma((nz - 1,)),
            dma, dma, dma((nz - 1,)), dma((nz - 1,)), dma, dma,
            dma((nz - 1,)), dma((nz - 1,)), dma((nz,)), dma((nz,)),
            dma((n // 2,)),
        ],
        compiler_params=pltpu.CompilerParams(
            collective_id=0, has_side_effects=True, vmem_limit_bytes=60 * 1024 * 1024),
        cost_estimate=pl.CostEstimate(
            flops=12 * bd * bd * cols, bytes_accessed=8 * bd * cols, transcendentals=0),
    )(orbitals)


def shards(orbitals):
    bd, cols = orbitals.shape
    nr = lax.axis_size("grid")
    fits = nr % 2 == 0 and nr >= 4 and bd % (4 * nr) == 0 and cols % 256 == 0 and cols >= 2048 // 2
    if lax.axis_size("band") == 4 and fits:
        return paired_shards(orbitals)
    return general_shards(orbitals)


def solution(mesh):
    return jax.shard_map(
        shards,
        mesh=mesh,
        in_specs=(P("band", "grid"),),
        out_specs=P("band", "grid"),
        check_vma=False,
    )
```

```python
import functools

import jax
import jax.numpy as jnp
from jax import lax
from jax.experimental import pallas as pl
from jax.experimental.pallas import tpu as pltpu
from jax.sharding import PartitionSpec as P

MESH = pl.DeviceIdType.MESH
NT = (((1,), (1,)), ((), ()))
NN = (((1,), (0,)), ((), ()))


def passed_along(block, axis, distance):
    devices = range(lax.axis_size(axis))
    route = [((i - distance) % len(devices), i) for i in devices]
    return lax.ppermute(block, axis, route)


def product(left, right):
    return jnp.dot(left, right, precision=lax.Precision.HIGHEST, preferred_element_type=jnp.float32)


def general_shards(orbitals):
    band_count = lax.axis_size("band")
    shifts = min(4, (band_count - 1) // 2)
    points = orbitals.shape[1] * lax.axis_size("grid")
    others = []
    for distance in range(1, shifts + 1):
        others.append(passed_along(orbitals, "band", distance))
    neighbours = [orbitals] + others
    partials = [product(orbitals, other.T) for other in neighbours]
    tiles = [lax.psum(partial_value, "grid") / points for partial_value in partials]
    identity = jnp.eye(orbitals.shape[0], dtype=jnp.float32)
    fix = product(tiles[0] - identity, orbitals)
    terms = [None]
    for distance in range(1, shifts + 1):
        fix = fix + product(tiles[distance], others[distance - 1])
        terms.append(product(tiles[distance].T, orbitals))
    for distance in range(1, shifts + 1):
        fix = fix + passed_along(terms[distance], "band", -distance)
    return orbitals - 0.5 * fix


def split(a):
    hi = a.astype(jnp.bfloat16)
    return hi, (a - hi.astype(jnp.float32)).astype(jnp.bfloat16)


def mm(a, b, dims):
    dot = functools.partial(lax.dot_general, dimension_numbers=dims, preferred_element_type=jnp.float32)
    return dot(a[0], b[0]) + (dot(a[0], b[1]) + dot(a[1], b[0]))


def kernel(
    nr, width, depth, x_ref, o_ref,
    blocks, dpart, dcore, drs, dred, dfull, tpart, tcore, trs, tred, tpair, tfull, fix,
    own_sem, xs, xr, ys, yr, dcs, dcr, drss, drsr, dags, dagr, cs, cr, rss, rsr, ps, pr, ags, agr, fs, fr, os,
):
    bd, cols = x_ref.shape
    nz = nr // 2
    points = cols * nr
    half = cols // 2
    n = cols // width
    nh = n // 2
    g = lax.axis_index("band")
    r = lax.axis_index("grid")
    z, core = r // 2, r % 2
    par = g % 2
    xn, yn, dn = g + 1 - 2 * par, (g + 2) % 4, 3 - g
    mate = z * 2 + (1 - core)
    partner = xn * (1 - core) + dn * core

    own_copy = pltpu.make_async_copy(x_ref, blocks.at[pl.ds(0, bd)], own_sem)
    own_copy.start()

    barrier = pltpu.get_barrier_semaphore()
    for peer in (xn, yn, dn):
        pl.semaphore_signal(barrier, inc=1, device_id={"band": peer}, device_id_type=MESH)
    pl.semaphore_signal(barrier, inc=1, device_id={"grid": mate}, device_id_type=MESH)
    for k in range(1, nz):
        pl.semaphore_signal(
            barrier, inc=1, device_id={"grid": lax.rem(z + k, nz) * 2 + core}, device_id_type=MESH)
    pl.semaphore_wait(barrier, 4 + nz - 1)

    def columns(c, parity):
        start = parity * half + c * width
        start = lax.rem(start, cols)
        return pl.ds(pl.multiple_of(start, 128), width)

    def remote(src, dst, send, recv, where):
        return pltpu.make_async_remote_copy(
            src_ref=src, dst_ref=dst, send_sem=send, recv_sem=recv, device_id=where, device_id_type=MESH)

    def x_send(c):
        at = columns(c, 1 - par)
        return remote(x_ref.at[:, at], blocks.at[pl.ds(bd, bd), at], xs.at[c], xr.at[c], {"band": xn})

    def x_recv(c):
        at = columns(c, par)
        return remote(x_ref.at[:, at], blocks.at[pl.ds(bd, bd), at], xs.at[c], xr.at[c], {"band": xn})

    def y_copy(c):
        at = columns(c, par)
        return remote(blocks.at[pl.ds(bd, bd), at], blocks.at[pl.ds(2 * bd, bd), at], ys.at[c], yr.at[c], {"band": yn})

    for c in range(min(depth, n)):
        x_send(c).start()

    own_copy.wait()

    def step_x(c):
        x_recv(c).wait_recv()
        y_copy(c).start()
        x_send(c).wait_send()
        if c + depth < n:
            x_send(c + depth).start()

    mine = split(blocks[pl.ds(0, bd), :])
    dpart[...] = mm(mine, mine, NT).reshape(nz, bd // nz, bd)

    def other_z(k):
        return lax.rem(z + k, nz)

    def to_z(k):
        return {"grid": other_z(k) * 2 + core}

    def drs_copy(k):
        return remote(dcore.at[other_z(k)], drs.at[k - 1], drss.at[k - 1], drsr.at[k - 1], to_z(k))

    def dag_copy(k):
        return remote(dred, dfull.at[z], dags.at[k - 1], dagr.at[k - 1], to_z(k))

    def dag_arrival(k):
        return remote(dred, dfull.at[lax.rem(z + nz - k, nz)], dags.at[k - 1], dagr.at[k - 1], to_z(k))

    dcore_copy = remote(dpart, dcore, dcs, dcr, {"grid": mate})
    dcore_copy.start()

    def add_tile(which, c):
        at = columns(c, par)
        a = split(blocks[pl.ds(0, bd), at])
        b = split(blocks[pl.ds((1 + which) * bd, bd), at])

        @pl.when(par == 0)
        def _():
            value = mm(a, b, NT).reshape(nz, bd // nz, bd)
            tpart[which] = value if c == 0 else tpart[which] + value

        @pl.when(par == 1)
        def _():
            value = mm(b, a, NT).reshape(nz, bd // nz, bd)
            tpart[which] = value if c == 0 else tpart[which] + value

    for c in range(nh):
        step_x(c)
        add_tile(0, c)
        if c >= 1:
            y_copy(c - 1).wait_recv()
            add_tile(1, c - 1)
        if c == 0:
            dcore_copy.wait()
            dcore[...] = dcore[...] + dpart[...]
            for k in range(1, nz):
                drs_copy(k).start()
        if c == 2:
            for k in range(1, nz):
                drs_copy(k).wait_recv()
            total = dcore[z]
            for k in range(1, nz):
                total = total + drs[k - 1]
            dred[...] = total
            dfull[z] = total
            for k in range(1, nz):
                dag_copy(k).start()

    core_copy = remote(tpart.at[1 - core], tcore, cs, cr, {"grid": mate})
    pair_copy = remote(tred, tpair, ps, pr, {"band": partner})

    def rs_copy(k):
        return remote(tcore.at[other_z(k)], trs.at[k - 1], rss.at[k - 1], rsr.at[k - 1], to_z(k))

    def ag_copy(k):
        return remote(tfull.at[core, z], tfull.at[core, z], ags.at[k - 1], agr.at[k - 1], {"grid": other_z(k) * 2 + core})

    def ag_arrival(k):
        at = tfull.at[core, lax.rem(z + nz - k, nz)]
        return remote(at, at, ags.at[k - 1], agr.at[k - 1], {"grid": other_z(k) * 2 + core})

    def mate_copy(k):
        at = tfull.at[core, lax.rem(z + nz - k, nz)]
        return remote(at, at, fs.at[k], fr.at[k], {"grid": mate})

    def mate_arrival(k):
        at = tfull.at[1 - core, lax.rem(z + nz - k, nz)]
        return remote(at, at, fs.at[k], fr.at[k], {"grid": mate})

    def on(which, stage):
        @pl.when(core == which)
        def _():
            stage()

    def sum_cores():
        core_copy.wait_recv()
        tcore[...] = tcore[...] + tpart[core]
        for k in range(1, nz):
            rs_copy(k).start()

    def sum_z():
        for k in range(1, nz):
            rs_copy(k).wait_recv()
        total = tcore[z]
        for k in range(1, nz):
            total = total + trs[k - 1]
        tred[...] = total
        pair_copy.start()

    def sum_pair():
        pair_copy.wait_recv()
        tfull[core, z] = tred[...] + tpair[...]
        for k in range(1, nz):
            ag_copy(k).start()
        mate_copy(0).start()

    def pass_on():
        for k in range(1, nz):
            ag_arrival(k).wait_recv()
            mate_copy(k).start()

    def from_mate():
        for k in range(nz):
            mate_arrival(k).wait_recv()

    on(1, core_copy.start)
    on(0, sum_cores)
    step_x(nh)
    y_copy(nh - 1).wait_recv()
    add_tile(1, nh - 1)
    on(0, core_copy.start)
    on(1, sum_cores)
    on(0, sum_z)
    for c in range(nh + 1, nh + 4):
        if c < n:
            step_x(c)
    on(0, sum_pair)
    for c in range(nh + 4, n - 1):
        step_x(c)
    on(1, sum_z)
    for c in range(max(n - 1, nh + 4), n):
        step_x(c)
    on(1, sum_pair)

    for k in range(1, nz):
        dag_arrival(k).wait_recv()
    scale = -0.5 / points
    wide = 2 * width
    steps = [pl.ds(t * wide, wide) for t in range(cols // wide)]
    on(0, pass_on)
    own_w = split(dfull[...].reshape(bd, bd) * scale)
    for at in steps:
        a = blocks[pl.ds(0, bd), at]
        fix[:, at] = 1.5 * a + mm(own_w, split(a), NN)
    core_copy.wait_send()

    def weights(which):
        @pl.when(par == 1)
        def _():
            tpart[which] = tfull[which].reshape(bd, bd).T.reshape(nz, bd // nz, bd)

        @pl.when(par == 0)
        def _():
            tpart[which] = tfull[which]

        return split(tpart[which].reshape(bd, bd) * scale)

    on(1, from_mate)
    w0 = weights(0)
    for at in steps:
        fix[:, at] = fix[:, at] + mm(w0, split(blocks[pl.ds(bd, bd), at]), NN)

    on(1, pass_on)
    for c in range(nh, n):
        y_copy(c).wait_recv()
    on(0, from_mate)
    w1 = weights(1)
    outs = []
    for t, at in enumerate(steps):
        fix[:, at] = fix[:, at] + mm(w1, split(blocks[pl.ds(2 * bd, bd), at]), NN)
        outs.append(pltpu.make_async_copy(fix.at[:, at], o_ref.at[:, at], os.at[t]))
        outs[-1].start()

    for c in range(n):
        y_copy(c).wait_send()
    pair_copy.wait_send()
    for k in range(1, nz):
        drs_copy(k).wait_send()
        dag_copy(k).wait_send()
        rs_copy(k).wait_send()
        ag_copy(k).wait_send()
    for k in range(nz):
        mate_copy(k).wait_send()
    for copy in outs:
        copy.wait()


def paired_shards(orbitals):
    bd, cols = orbitals.shape
    nr = lax.axis_size("grid")
    nz = nr // 2
    width = 128
    n = cols // width
    f32 = jnp.float32
    dma = pltpu.SemaphoreType.DMA
    part = bd // nz
    return pl.pallas_call(
        functools.partial(kernel, nr, width, 3),
        out_shape=jax.ShapeDtypeStruct((bd, cols), f32),
        in_specs=[pl.BlockSpec(memory_space=pl.ANY)],
        out_specs=pl.BlockSpec(memory_space=pl.ANY),
        scratch_shapes=[
            pltpu.VMEM((3 * bd, cols), f32),
            pltpu.VMEM((nz, part, bd), f32),
            pltpu.VMEM((nz, part, bd), f32),
            pltpu.VMEM((nz - 1, part, bd), f32),
            pltpu.VMEM((part, bd), f32),
            pltpu.VMEM((nz, part, bd), f32),
            pltpu.VMEM((2, nz, part, bd), f32),
            pltpu.VMEM((nz, part, bd), f32),
            pltpu.VMEM((nz - 1, part, bd), f32),
            pltpu.VMEM((part, bd), f32),
            pltpu.VMEM((part, bd), f32),
            pltpu.VMEM((2, nz, part, bd), f32),
            pltpu.VMEM((bd, cols), f32),
            dma, dma((n,)), dma((n,)), dma((n,)), dma((n,)),
            dma, dma, dma((nz - 1,)), dma((nz - 1,)), dma((nz - 1,)), dma((nz - 1,)),
            dma, dma, dma((nz - 1,)), dma((nz - 1,)), dma, dma,
            dma((nz - 1,)), dma((nz - 1,)), dma((nz,)), dma((nz,)),
            dma((n // 2,)),
        ],
        compiler_params=pltpu.CompilerParams(
            collective_id=0, has_side_effects=True, vmem_limit_bytes=105 * 512 * 1024),
        cost_estimate=pl.CostEstimate(
            flops=12 * bd * bd * cols, bytes_accessed=8 * bd * cols, transcendentals=0),
    )(orbitals)


def shards(orbitals):
    bd, cols = orbitals.shape
    nr = lax.axis_size("grid")
    fits = nr % 2 == 0 and nr >= 4 and bd % (4 * nr) == 0 and cols % 256 == 0 and cols >= 2048 // 2
    if lax.axis_size("band") == 4 and fits:
        return paired_shards(orbitals)
    return general_shards(orbitals)


def solution(mesh):
    return jax.shard_map(
        shards,
        mesh=mesh,
        in_specs=(P("band", "grid"),),
        out_specs=P("band", "grid"),
        check_vma=False,
    )
```

```python
import functools

import jax
import jax.numpy as jnp
from jax import lax
from jax.experimental import pallas as pl
from jax.experimental.pallas import tpu as pltpu
from jax.sharding import PartitionSpec as P

MESH = pl.DeviceIdType.MESH
NT = (((1,), (1,)), ((), ()))
NN = (((1,), (0,)), ((), ()))


def passed_along(block, axis, distance):
    devices = range(lax.axis_size(axis))
    route = [((i - distance) % len(devices), i) for i in devices]
    return lax.ppermute(block, axis, route)


def product(left, right):
    return jnp.dot(left, right, precision=lax.Precision.HIGHEST, preferred_element_type=jnp.float32)


def general_shards(orbitals):
    band_count = lax.axis_size("band")
    shifts = min(4, (band_count - 1) // 2)
    points = orbitals.shape[1] * lax.axis_size("grid")
    others = []
    for distance in range(1, shifts + 1):
        others.append(passed_along(orbitals, "band", distance))
    neighbours = [orbitals] + others
    partials = [product(orbitals, other.T) for other in neighbours]
    tiles = [lax.psum(partial_value, "grid") / points for partial_value in partials]
    identity = jnp.eye(orbitals.shape[0], dtype=jnp.float32)
    fix = product(tiles[0] - identity, orbitals)
    terms = [None]
    for distance in range(1, shifts + 1):
        fix = fix + product(tiles[distance], others[distance - 1])
        terms.append(product(tiles[distance].T, orbitals))
    for distance in range(1, shifts + 1):
        fix = fix + passed_along(terms[distance], "band", -distance)
    return orbitals - 0.5 * fix


def split(a):
    hi = a.astype(jnp.bfloat16)
    return hi, (a - hi.astype(jnp.float32)).astype(jnp.bfloat16)


def mm(a, b, dims):
    dot = functools.partial(lax.dot_general, dimension_numbers=dims, preferred_element_type=jnp.float32)
    return dot(a[0], b[0]) + (dot(a[0], b[1]) + dot(a[1], b[0]))


def kernel(
    nr, width, depth, x_ref, o_ref,
    blocks, dpart, dcore, drs, dred, dfull, tpart, tcore, trs, tred, tpair, tfull, fix,
    own_sem, xs, xr, ys, yr, dcs, dcr, drss, drsr, dags, dagr, cs, cr, rss, rsr, ps, pr, ags, agr, fs, fr, os,
):
    bd, cols = x_ref.shape
    nz = nr // 2
    points = cols * nr
    half = cols // 2
    n = cols // width
    nh = n // 2
    g = lax.axis_index("band")
    r = lax.axis_index("grid")
    z, core = r // 2, r % 2
    par = g % 2
    xn, yn, dn = g + 1 - 2 * par, (g + 2) % 4, 3 - g
    mate = z * 2 + (1 - core)
    partner = xn * (1 - core) + dn * core

    own_copy = pltpu.make_async_copy(x_ref, blocks.at[pl.ds(0, bd)], own_sem)
    own_copy.start()

    barrier = pltpu.get_barrier_semaphore()
    for k in range(1, nz):
        pl.semaphore_signal(
            barrier, inc=1, device_id={"grid": lax.rem(z + k, nz) * 2 + core}, device_id_type=MESH)
    for peer in (dn, yn, xn):
        pl.semaphore_signal(barrier, inc=1, device_id={"band": peer}, device_id_type=MESH)
    pl.semaphore_signal(barrier, inc=1, device_id={"grid": mate}, device_id_type=MESH)
    pl.semaphore_wait(barrier, 4 + nz - 1)

    def columns(c, parity):
        start = parity * half + c * width
        start = lax.rem(start, cols)
        return pl.ds(pl.multiple_of(start, 128), width)

    def remote(src, dst, send, recv, where):
        return pltpu.make_async_remote_copy(
            src_ref=src, dst_ref=dst, send_sem=send, recv_sem=recv, device_id=where, device_id_type=MESH)

    def x_send(c):
        at = columns(c, 1 - par)
        return remote(x_ref.at[:, at], blocks.at[pl.ds(bd, bd), at], xs.at[c], xr.at[c], {"band": xn})

    def x_recv(c):
        at = columns(c, par)
        return remote(x_ref.at[:, at], blocks.at[pl.ds(bd, bd), at], xs.at[c], xr.at[c], {"band": xn})

    def y_copy(c):
        at = columns(c, par)
        return remote(blocks.at[pl.ds(bd, bd), at], blocks.at[pl.ds(2 * bd, bd), at], ys.at[c], yr.at[c], {"band": yn})

    for c in range(min(depth, n)):
        x_send(c).start()

    own_copy.wait()

    def step_x(c):
        x_recv(c).wait_recv()
        y_copy(c).start()
        x_send(c).wait_send()
        if c + depth < n:
            x_send(c + depth).start()

    mine = split(blocks[pl.ds(0, bd), :])
    dpart[...] = mm(mine, mine, NT).reshape(nz, bd // nz, bd)

    def other_z(k):
        return lax.rem(z + k, nz)

    def to_z(k):
        return {"grid": other_z(k) * 2 + core}

    def drs_copy(k):
        return remote(dcore.at[other_z(k)], drs.at[k - 1], drss.at[k - 1], drsr.at[k - 1], to_z(k))

    def dag_copy(k):
        return remote(dred, dfull.at[z], dags.at[k - 1], dagr.at[k - 1], to_z(k))

    def dag_arrival(k):
        return remote(dred, dfull.at[lax.rem(z + nz - k, nz)], dags.at[k - 1], dagr.at[k - 1], to_z(k))

    dcore_copy = remote(dpart, dcore, dcs, dcr, {"grid": mate})
    dcore_copy.start()

    def add_tile(which, c):
        at = columns(c, par)
        a = split(blocks[pl.ds(0, bd), at])
        b = split(blocks[pl.ds((1 + which) * bd, bd), at])

        @pl.when(par == 0)
        def _():
            value = mm(a, b, NT).reshape(nz, bd // nz, bd)
            tpart[which] = value if c == 0 else tpart[which] + value

        @pl.when(par == 1)
        def _():
            value = mm(b, a, NT).reshape(nz, bd // nz, bd)
            tpart[which] = value if c == 0 else tpart[which] + value

    for c in range(nh):
        step_x(c)
        add_tile(0, c)
        if c >= 1:
            y_copy(c - 1).wait_recv()
            add_tile(1, c - 1)
        if c == 0:
            dcore_copy.wait()
            dcore[...] = dcore[...] + dpart[...]
            for k in range(1, nz):
                drs_copy(k).start()
        if c == 2:
            for k in range(1, nz):
                drs_copy(k).wait_recv()
            total = dcore[z]
            for k in range(1, nz):
                total = total + drs[k - 1]
            dred[...] = total
            dfull[z] = total
            for k in range(1, nz):
                dag_copy(k).start()

    core_copy = remote(tpart.at[1 - core], tcore, cs, cr, {"grid": mate})
    pair_copy = remote(tred, tpair, ps, pr, {"band": partner})

    def rs_copy(k):
        return remote(tcore.at[other_z(k)], trs.at[k - 1], rss.at[k - 1], rsr.at[k - 1], to_z(k))

    def ag_copy(k):
        return remote(tfull.at[core, z], tfull.at[core, z], ags.at[k - 1], agr.at[k - 1], {"grid": other_z(k) * 2 + core})

    def ag_arrival(k):
        at = tfull.at[core, lax.rem(z + nz - k, nz)]
        return remote(at, at, ags.at[k - 1], agr.at[k - 1], {"grid": other_z(k) * 2 + core})

    def mate_copy(k):
        at = tfull.at[core, lax.rem(z + nz - k, nz)]
        return remote(at, at, fs.at[k], fr.at[k], {"grid": mate})

    def mate_arrival(k):
        at = tfull.at[1 - core, lax.rem(z + nz - k, nz)]
        return remote(at, at, fs.at[k], fr.at[k], {"grid": mate})

    def on(which, stage):
        @pl.when(core == which)
        def _():
            stage()

    def sum_cores():
        core_copy.wait_recv()
        tcore[...] = tcore[...] + tpart[core]
        for k in range(1, nz):
            rs_copy(k).start()

    def sum_z():
        for k in range(1, nz):
            rs_copy(k).wait_recv()
        total = tcore[z]
        for k in range(1, nz):
            total = total + trs[k - 1]
        tred[...] = total
        pair_copy.start()

    def sum_pair():
        pair_copy.wait_recv()
        tfull[core, z] = tred[...] + tpair[...]
        for k in range(1, nz):
            ag_copy(k).start()
        mate_copy(0).start()

    def pass_on():
        for k in range(1, nz):
            ag_arrival(k).wait_recv()
            mate_copy(k).start()

    def from_mate():
        for k in range(nz):
            mate_arrival(k).wait_recv()

    on(1, core_copy.start)
    on(0, sum_cores)
    step_x(nh)
    y_copy(nh - 1).wait_recv()
    add_tile(1, nh - 1)
    on(0, core_copy.start)
    on(1, sum_cores)
    on(0, sum_z)
    for c in range(nh + 1, nh + 4):
        if c < n:
            step_x(c)
    on(0, sum_pair)
    for c in range(nh + 4, n - 1):
        step_x(c)
    on(1, sum_z)
    for c in range(max(n - 1, nh + 4), n):
        step_x(c)
    on(1, sum_pair)

    for k in range(1, nz):
        dag_arrival(k).wait_recv()
    scale = -0.5 / points
    wide = 2 * width
    steps = [pl.ds(t * wide, wide) for t in range(cols // wide)]
    on(0, pass_on)
    own_w = split(dfull[...].reshape(bd, bd) * scale)
    for at in steps:
        a = blocks[pl.ds(0, bd), at]
        fix[:, at] = 1.5 * a + mm(own_w, split(a), NN)
    core_copy.wait_send()

    def weights(which):
        @pl.when(par == 1)
        def _():
            tpart[which] = tfull[which].reshape(bd, bd).T.reshape(nz, bd // nz, bd)

        @pl.when(par == 0)
        def _():
            tpart[which] = tfull[which]

        return split(tpart[which].reshape(bd, bd) * scale)

    on(1, from_mate)
    w0 = weights(0)
    for at in steps:
        fix[:, at] = fix[:, at] + mm(w0, split(blocks[pl.ds(bd, bd), at]), NN)

    on(1, pass_on)
    for c in range(nh, n):
        y_copy(c).wait_recv()
    on(0, from_mate)
    w1 = weights(1)
    outs = []
    for t, at in enumerate(steps):
        fix[:, at] = fix[:, at] + mm(w1, split(blocks[pl.ds(2 * bd, bd), at]), NN)
        outs.append(pltpu.make_async_copy(fix.at[:, at], o_ref.at[:, at], os.at[t]))
        outs[-1].start()

    for c in range(n):
        y_copy(c).wait_send()
    pair_copy.wait_send()
    for k in range(1, nz):
        drs_copy(k).wait_send()
        dag_copy(k).wait_send()
        rs_copy(k).wait_send()
        ag_copy(k).wait_send()
    for k in range(nz):
        mate_copy(k).wait_send()
    for copy in outs:
        copy.wait()


def paired_shards(orbitals):
    bd, cols = orbitals.shape
    nr = lax.axis_size("grid")
    nz = nr // 2
    width = 128
    n = cols // width
    f32 = jnp.float32
    dma = pltpu.SemaphoreType.DMA
    part = bd // nz
    return pl.pallas_call(
        functools.partial(kernel, nr, width, 3),
        out_shape=jax.ShapeDtypeStruct((bd, cols), f32),
        in_specs=[pl.BlockSpec(memory_space=pl.ANY)],
        out_specs=pl.BlockSpec(memory_space=pl.ANY),
        scratch_shapes=[
            pltpu.VMEM((3 * bd, cols), f32),
            pltpu.VMEM((nz, part, bd), f32),
            pltpu.VMEM((nz, part, bd), f32),
            pltpu.VMEM((nz - 1, part, bd), f32),
            pltpu.VMEM((part, bd), f32),
            pltpu.VMEM((nz, part, bd), f32),
            pltpu.VMEM((2, nz, part, bd), f32),
            pltpu.VMEM((nz, part, bd), f32),
            pltpu.VMEM((nz - 1, part, bd), f32),
            pltpu.VMEM((part, bd), f32),
            pltpu.VMEM((part, bd), f32),
            pltpu.VMEM((2, nz, part, bd), f32),
            pltpu.VMEM((bd, cols), f32),
            dma, dma((n,)), dma((n,)), dma((n,)), dma((n,)),
            dma, dma, dma((nz - 1,)), dma((nz - 1,)), dma((nz - 1,)), dma((nz - 1,)),
            dma, dma, dma((nz - 1,)), dma((nz - 1,)), dma, dma,
            dma((nz - 1,)), dma((nz - 1,)), dma((nz,)), dma((nz,)),
            dma((n // 2,)),
        ],
        compiler_params=pltpu.CompilerParams(
            collective_id=0, has_side_effects=True, vmem_limit_bytes=105 * 512 * 1024),
        cost_estimate=pl.CostEstimate(
            flops=12 * bd * bd * cols, bytes_accessed=8 * bd * cols, transcendentals=0),
    )(orbitals)


def shards(orbitals):
    bd, cols = orbitals.shape
    nr = lax.axis_size("grid")
    fits = nr % 2 == 0 and nr >= 4 and bd % (4 * nr) == 0 and cols % 256 == 0 and cols >= 2048 // 2
    if lax.axis_size("band") == 4 and fits:
        return paired_shards(orbitals)
    return general_shards(orbitals)


def solution(mesh):
    return jax.shard_map(
        shards,
        mesh=mesh,
        in_specs=(P("band", "grid"),),
        out_specs=P("band", "grid"),
        check_vma=False,
    )
```
